128 devices in a mesh: dp: 8 (over z, core), seq: 16 (over y, x).
Axes of the slice: x: 4, y: 4, z: 4, core: 2. Of those that a mesh axis runs over, the one named last changes fastest.
Arguments:
- video_projected: bfloat16 [8, 3072, 3, 4096], P('dp', 'seq'), may hold values from -6 to 6
- text_projected: bfloat16 [8, 256, 3, 4096], P('dp', 'seq'), may hold values from -6 to 6
- head_live: int32 [32], replicated, may hold values from 0 to 1, as said below
- text_valid: int32 [8, 256], P('dp'), may hold values from 0 to 1, as said below
- text_weight: bfloat16 [4096, 3072], P('seq', 'dp'), may hold values from -0.109375 to 0.109375
- text_cotangent: bfloat16 [8, 256, 3072], P('dp', 'seq'), may hold values from -6 to 6
Outputs:
- video_attended: bfloat16 [8, 3072, 4096], P('dp', 'seq')
- text_output: bfloat16 [8, 256, 3072], P('dp', 'seq')
- weight_gradient: float32 [4096, 3072], P('seq', 'dp')
The draws below stay inside these ranges and needn't reach their ends.
Inputs may be any that keep to these rules, and one draw needn't show every extreme that they name: `head_live`: exactly 24 entries are 1. `text_valid`: in each window the valid text tokens are a prefix of 64 or more tokens.
All inputs are finite; a program needn't handle non-finite values.
Results may differ from the reference program's by a relative error of at most 0.0057.
Values may be sent and summed in bfloat16 or wider, within the bound.
No kernel may reach another device: no remote copies, remote signals or barrier semaphores. Data moves between devices by JAX's collectives and lax.ppermute only.
A program may use at most 128 MiB of HBM per device.

```python
import jax
import jax.numpy as jnp
from jax import lax

D = 3072
HEADS = 24
HD = 128
HP = 32
WIN = 8
VID = 3072
TXT = 256


def draw_video_projected(key, part):
    key = jax.random.fold_in(key, 11)
    return jax.random.truncated_normal(key, -6.0, 6.0, (WIN, VID, 3, HP * HD), jnp.float32).astype(jnp.bfloat16)


def draw_text_projected(key, part):
    key = jax.random.fold_in(key, 23)
    return jax.random.truncated_normal(key, -6.0, 6.0, (WIN, TXT, 3, HP * HD), jnp.float32).astype(jnp.bfloat16)


def draw_head_live(key, part):
    key = jax.random.fold_in(key, 37)
    order = jax.random.permutation(key, HP)
    return (order < HEADS).astype(jnp.int32)


def draw_text_valid(key, part):
    key = jax.random.fold_in(key, 41)
    lengths = jax.random.randint(key, (WIN, 1), TXT // 4, TXT + 1)
    return (jnp.arange(TXT)[None, :] < lengths).astype(jnp.int32)


def levels(key, shape, cuts, low, largest):
    gain, own = 1.0, jax.random.fold_in(key, 6)
    for dim, blocks in cuts:
        steps = jnp.exp(jax.random.uniform(jax.random.fold_in(own, dim), (blocks,), jnp.float32, low / len(cuts), largest / len(cuts)))
        gain = gain * jnp.repeat(steps, shape[dim] // blocks).reshape([-1 if axis == dim else 1 for axis in range(len(shape))])
    return gain


def centred(stream_key, dims, scale, bound, cuts=(), held_as=jnp.bfloat16):
    gain = levels(stream_key, dims, cuts, -0.22, 0.18) if cuts else 1.0
    entries = jax.random.normal(stream_key, dims, jnp.float32) * scale * gain
    return jnp.minimum(jnp.maximum(entries, -bound), bound).astype(held_as)


def setup_inputs(seed: int = 0) -> dict:
    splits = jax.random.split(jax.random.key(seed), 7)
    return {
        "video_projected": draw_video_projected(jax.random.fold_in(splits[6], 71), 0),
        "text_projected": draw_text_projected(jax.random.fold_in(splits[6], 71), 0),
        "head_live": draw_head_live(jax.random.fold_in(splits[6], 71), 0),
        "text_valid": draw_text_valid(jax.random.fold_in(splits[6], 71), 0),
        "text_weight": centred(splits[4], (HP * HD, D), (HEADS * HD) ** -0.5, 0.109375, ((0, 16), (1, 8))),
        "text_cotangent": centred(splits[5], (WIN, TXT, D), 1.0, 6.0, ((0, 8), (1, 16))),
    }


def head_attend(queries, key_rows, value_rows, key_ok, live):
    scale = 1.0 / (HD ** 0.5)
    blocks = queries.reshape(4, queries.shape[0] // 4, queries.shape[1])

    def one_block(block):
        scores = jnp.dot(block, key_rows.T, preferred_element_type=jnp.float32) * scale
        scores = jnp.where(key_ok[None, :], scores, jnp.float32(-1e30))
        highest = jnp.max(scores, axis=1, keepdims=True)
        expos = jnp.exp(scores - highest)
        weights = (expos / jnp.sum(expos, axis=1, keepdims=True)).astype(jnp.bfloat16)
        result = jnp.dot(weights, value_rows, preferred_element_type=jnp.float32)
        return (result * live).astype(jnp.bfloat16)

    return lax.map(one_block, blocks).reshape(queries.shape[0], queries.shape[1])


def reference(video_projected, text_projected, head_live, text_valid, text_weight, text_cotangent):
    live_all = head_live.astype(jnp.float32)

    def one_window(inputs):
        video, text, valid, cotangent = inputs
        joined = jnp.concatenate([video, text], axis=0)
        length = joined.shape[0]
        key_ok = jnp.concatenate([jnp.ones((video.shape[0],), bool), valid > 0])
        split = joined.reshape(length, 3, HP, HD).transpose(1, 2, 0, 3)

        def one_head(args):
            queries, key_rows, value_rows, live = args
            return head_attend(queries, key_rows, value_rows, key_ok, live)

        heads = lax.map(one_head, (split[0], split[1], split[2], live_all))
        attended = heads.transpose(1, 0, 2).reshape(length, HP * HD)
        text_rows = attended[video.shape[0]:]
        output = jnp.dot(text_rows, text_weight, preferred_element_type=jnp.float32).astype(jnp.bfloat16)
        term = jnp.dot(text_rows.T, cotangent, preferred_element_type=jnp.float32)
        return attended[:video.shape[0]], output, term

    video_out, text_out, terms = lax.map(one_window, (video_projected, text_projected, text_valid, text_cotangent))
    return video_out, text_out, jnp.sum(terms, axis=0)
```

```python
import functools

import numpy as np

import jax
import jax.numpy as jnp
from jax import lax
from jax.experimental import pallas as pl
from jax.experimental.pallas import tpu as pltpu
from jax.sharding import PartitionSpec as P

HD = 128
LIVE = 24
SLOTS = 32
N = 3328
VID = 3072
TXT = 256
SEQ = 16
VT = 192
TT = 16
HALF = 96
ROWS = VT + TT + HALF + TT
CHUNK = 256
SCALE = float(np.log2(np.e) / HD**0.5)
BF16 = jnp.bfloat16
F32 = jnp.float32
VMEM = pl.BlockSpec(memory_space=pltpu.VMEM)
SMEM = pl.BlockSpec(memory_space=pltpu.SMEM)
ANY = pl.BlockSpec(memory_space=pl.ANY)


def run_all(copies):
    for copy in copies:
        copy.start()
    for copy in copies:
        copy.wait()


def head_columns(slots, rank):
    return pl.ds(pl.multiple_of(slots[rank] * HD, HD), HD)


def give_kernel(slots, core, video, text, give, sem):
    start = pl.multiple_of((1 - core[0]) * HALF, 16)
    copies = []
    for j in range(8):
        cols = head_columns(slots, 16 + j)
        copies.append(pltpu.make_async_copy(
            video.at[:, pl.ds(start, HALF), cols], give.at[j, :, pl.ds(0, HALF), :], sem.at[0]))
        copies.append(pltpu.make_async_copy(
            text.at[:, :, cols], give.at[j, :, pl.ds(HALF, TT), :], sem.at[1]))
    run_all(copies)


def pack_kernel(slots, core, video, text, buf, sem):
    start = pl.multiple_of(core[0] * HALF, 16)
    copies = []
    for r in range(16):
        cols = head_columns(slots, r)
        copies.append(pltpu.make_async_copy(
            video.at[:, :, cols], buf.at[r, :, pl.ds(0, VT), :], sem.at[0]))
        copies.append(pltpu.make_async_copy(
            text.at[:, :, cols], buf.at[r, :, pl.ds(VT, TT), :], sem.at[1]))
    for j in range(8):
        cols = head_columns(slots, 16 + j)
        to = 2 * j + core[0]
        copies.append(pltpu.make_async_copy(
            video.at[:, pl.ds(start, HALF), cols], buf.at[to, :, pl.ds(VT + TT, HALF), :], sem.at[2]))
        copies.append(pltpu.make_async_copy(
            text.at[:, :, cols], buf.at[to, :, pl.ds(VT + TT + HALF, TT), :], sem.at[3]))
    run_all(copies)


def fill_kernel(core, got, _, buf, sem):
    copies = []
    for j in range(8):
        to = 2 * j + 1 - core[0]
        copies.append(pltpu.make_async_copy(
            got.at[j], buf.at[to, :, pl.ds(VT + TT, HALF + TT), :], sem.at[0]))
    run_all(copies)


def rows_dot(a, b):
    return lax.dot_general(a, b, (((1,), (1,)), ((), ())), preferred_element_type=F32)


def lay_a(recv, keys, values):
    for s in range(SEQ):
        keys[s * VT:(s + 1) * VT, :] = recv[s, 1, 0:VT, :]
        values[s * VT:(s + 1) * VT, 0:HD] = recv[s, 2, 0:VT, :]
        keys[VID + s * TT:VID + (s + 1) * TT, :] = recv[s, 1, VT:VT + TT, :]
        values[VID + s * TT:VID + (s + 1) * TT, 0:HD] = recv[s, 2, VT:VT + TT, :]
    values[:, HD:] = jnp.ones((N, HD), BF16)


def lay_c(recv, other, keys, values):
    first, tail = VT + TT, VT + TT + HALF
    for s in range(SEQ):
        at, far = s * HALF, VID // 2 + s * HALF
        keys[at:at + HALF, :] = recv[s, 1, first:tail, :]
        values[at:at + HALF, 0:HD] = recv[s, 2, first:tail, :]
        keys[far:far + HALF, :] = other[s, 0]
        values[far:far + HALF, 0:HD] = other[s, 1]
        keys[VID + s * TT:VID + (s + 1) * TT, :] = recv[s, 1, tail:ROWS, :]
        values[VID + s * TT:VID + (s + 1) * TT, 0:HD] = recv[s, 2, tail:ROWS, :]
    values[:, HD:] = jnp.ones((N, HD), BF16)


def score_chunk(query, keys, bias, scores, slot, c, top):
    rows = query.shape[0]
    s = rows_dot(query, keys[c:c + CHUNK, :])
    if c >= VID:
        s = s + bias[:, c - VID:c - VID + CHUNK]
    scores[slot, 0:rows, c:c + CHUNK] = s
    for t in range(0, CHUNK, HD):
        x = s[:, t:t + HD]
        top = x if top is None else jnp.maximum(top, x)
    return top


def keep_top(tops, slot, top):
    rows = top.shape[0]
    highest = jnp.max(top, axis=1, keepdims=True) * SCALE
    tops[slot, 0:rows, :] = jnp.broadcast_to(highest, (rows, HD))


def score_block(query, keys, bias, scores, tops, slot):
    top = None
    for c in range(0, N, CHUNK):
        top = score_chunk(query, keys, bias, scores, slot, c, top)
    keep_top(tops, slot, top)


def attend_block(rows, values, scores, tops, slot, following=None):
    highest = jnp.concatenate([tops[slot, 0:rows, :]] * (CHUNK // HD), axis=1)
    top, total = None, None
    for c in range(0, N, CHUNK):
        if following is not None:
            query, keys, bias = following
            top = score_chunk(query, keys, bias, scores, 1 - slot, c, top)
        p = jnp.exp2(scores[slot, 0:rows, c:c + CHUNK] * SCALE - highest)
        part = jnp.dot(p.astype(BF16), values[c:c + CHUNK, :], preferred_element_type=F32)
        total = part if total is None else total + part
    if following is not None:
        keep_top(tops, 1 - slot, top)
    return (total[:, 0:HD] / total[:, HD:]).astype(BF16)


def text_kernel(bias_a, bias_c, recv, other, _w, _c, out, scores, tops, keys_a, values_a, keys_c, values_c):
    lay_a(recv, keys_a, values_a)
    ba, bc = bias_a[...], bias_c[...]
    score_block(recv[:, 0, VT:VT + TT, :].reshape(TXT, HD), keys_a, ba, scores, tops, 0)
    lay_c(recv, other, keys_c, values_c)
    query = recv[:, 0, VT + TT + HALF:ROWS, :].reshape(TXT, HD)
    got = attend_block(TXT, values_a, scores, tops, 0, (query, keys_c, bc))
    out[:, 0:TT, :] = got.reshape(SEQ, TT, HD)
    got = attend_block(TXT, values_c, scores, tops, 1)
    out[:, TT:2 * TT, :] = got.reshape(SEQ, TT, HD)


def video_blocks(count, rows, load, store, keys, values, bias, scores, tops):
    def step(i, slot, more):
        following = (load(i + 1), keys, bias) if more else None
        store(i, attend_block(rows, values, scores, tops, slot, following))

    score_block(load(0), keys, bias, scores, tops, 0)

    def body(j, carry):
        step(2 * j, 0, True)
        step(2 * j + 1, 1, True)
        return carry

    lax.fori_loop(0, count // 2 - 1, body, 0)
    step(count - 2, 0, True)
    step(count - 1, 1, False)


def a_kernel(bias_a, recv, out, scores, tops, keys, values):
    lay_a(recv, keys, values)

    def load(i):
        return recv[pl.ds(2 * i, 2), 0, 0:VT, :].reshape(2 * VT, HD)

    def store(i, got):
        out[pl.ds(2 * i, 2)] = got.reshape(2, VT, HD)

    video_blocks(8, 2 * VT, load, store, keys, values, bias_a[...], scores, tops)


def c_kernel(bias_c, recv, other, out_a, out, scores, tops, keys, values):
    lay_c(recv, other, keys, values)
    out[:, 0:VT, :] = out_a[...]

    def load(i):
        return recv[pl.ds(4 * i, 4), 0, VT + TT:VT + TT + HALF, :].reshape(4 * HALF, HD)

    def store(i, got):
        out[pl.ds(4 * i, 4), VT:VT + HALF, :] = got.reshape(4, HALF, HD)

    video_blocks(4, 4 * HALF, load, store, keys, values, bias_c[...], scores, tops)


def slot_text_kernel(ranks, core, seat, got, _, out):
    for h in range(SLOTS):
        rank = ranks[h]
        group = (h // 8) ^ (seat[0] // 4)
        pair = ((h // 2) % 4) ^ (seat[0] % 4)
        cols = pl.ds(pl.multiple_of((pair * 2 + h % 2) * HD, HD), HD)

        @pl.when(rank < 0)
        def _():
            out[group, :, cols] = jnp.zeros((TT, HD), BF16)

        @pl.when((rank >= 0) & (rank < 16))
        def _():
            out[group, :, cols] = got[jnp.clip(rank, 0, 15), 0:TT, :]

        @pl.when(rank >= 16)
        def _():
            out[group, :, cols] = got[2 * jnp.clip(rank - 16, 0, 7) + core[0], TT:2 * TT, :]


def project_kernel(rows, weight, cot, p0, p1, p2, p3, g0, g1, g2, g3):
    part = jnp.dot(rows[...], weight[...], preferred_element_type=F32).reshape(8, 4, TT, 384)
    for j, ref in enumerate((p0, p1, p2, p3)):
        ref[...] = part[:, j].astype(ref.dtype)
    for j, ref in enumerate((g0, g1, g2, g3)):
        term = lax.dot_general(
            rows[:, j * 256:(j + 1) * 256], cot[...], (((0,), (0,)), ((), ())),
            preferred_element_type=F32)
        ref[...] = term.astype(ref.dtype)


def slot_video_kernel(ranks, core, got, other, out):
    mine = pl.multiple_of(core[0] * HALF, 16)
    far = pl.multiple_of((1 - core[0]) * HALF, 16)
    for h in range(SLOTS):
        rank = ranks[h]
        cols = pl.ds(h * HD, HD)

        @pl.when(rank < 0)
        def _():
            out[:, cols] = jnp.zeros((VT, HD), BF16)

        @pl.when((rank >= 0) & (rank < 16))
        def _():
            out[:, cols] = got[jnp.clip(rank, 0, 15), 0:VT, :]

        @pl.when(rank >= 16)
        def _():
            j = jnp.clip(rank - 16, 0, 7)
            out[pl.ds(mine, HALF), cols] = got[2 * j + core[0], VT:VT + HALF, :]
            out[pl.ds(far, HALF), cols] = other[j]


def shape(*dims, dtype=BF16):
    return jax.ShapeDtypeStruct(dims, dtype)


def cost(rows):
    return pl.CostEstimate(
        flops=4 * rows * N * HD, bytes_accessed=8 << 20, transcendentals=rows * N)


def attention_call(kernel, name, rows, block, heads, out_shape, specs):
    scratch = [pltpu.VMEM((2, block, N), F32), pltpu.VMEM((2, block, HD), F32)]
    for _ in range(heads):
        scratch += [pltpu.VMEM((N, HD), BF16), pltpu.VMEM((N, 2 * HD), BF16)]
    return pl.pallas_call(
        kernel, out_shape=out_shape, in_specs=specs, out_specs=VMEM, scratch_shapes=scratch,
        cost_estimate=cost(rows), name=name,
        compiler_params=pltpu.CompilerParams(vmem_limit_bytes=40 << 20))


def trade(x, axis, mask):
    count = 8 if axis == "dp" else SEQ
    return lax.ppermute(x, axis, [(i, i ^ mask) for i in range(count)])


def swap(x):
    return trade(x, "dp", 1)


def by_xor(x, index):
    count, rest = x.shape[0], x.shape[1:]
    bits = count.bit_length() - 1
    for b in range(bits):
        parts = x.reshape((count >> (b + 1), 2, 1 << b) + rest)
        x = jnp.where((index >> b) & 1 > 0, parts[:, ::-1], parts).reshape((count,) + rest)
    return x


def gather4(x, axis, low):
    near, far = trade(x, axis, low), trade(x, axis, 3 * low)
    half = x.shape[0] // 2
    opposite = jnp.concatenate(
        [trade(near[:half], axis, 3 * low), trade(far[half:], axis, low)], axis=0)
    return jnp.stack([x, near, opposite, far])


def gather_dp(x):
    along = gather4(x, "dp", 2)
    return jnp.stack([along, swap(along)], axis=1).reshape((8,) + x.shape)


def exchange_dp(x):
    rest = x.shape[1:]
    for b in (2, 1, 0):
        parts = x.reshape((8 >> (b + 1), 2, 1 << b) + rest)
        got = trade(parts[:, 1], "dp", 1 << b)
        x = jnp.stack([parts[:, 0], got], axis=1).reshape((8,) + rest)
    return x


def on_device(video_projected, text_projected, head_live, text_valid, text_weight, text_cotangent):
    video = video_projected[0].transpose(1, 0, 2)
    text = text_projected[0].transpose(1, 0, 2)
    seq = lax.axis_index("seq")
    dp = lax.axis_index("dp")
    core_bit = dp % 2
    core = core_bit.astype(jnp.int32).reshape(1)
    seat = seq.astype(jnp.int32).reshape(1)

    heads = jnp.arange(SLOTS, dtype=jnp.int32)
    live = head_live > 0
    place = jnp.sum(jnp.where(heads[None, :] < heads[:, None], head_live[None, :], 0), axis=1)
    ranks = jnp.where(live, place, -1).astype(jnp.int32)
    slots = jnp.sum(
        jnp.where(ranks[None, :] == jnp.arange(LIVE, dtype=jnp.int32)[:, None], heads[None, :], 0),
        axis=1).astype(jnp.int32)

    give = pl.pallas_call(
        give_kernel, out_shape=shape(8, 3, HALF + TT, HD), in_specs=[SMEM, SMEM, ANY, ANY],
        out_specs=VMEM, scratch_shapes=[pltpu.SemaphoreType.DMA((2,))], name="give",
        cost_estimate=pl.CostEstimate(flops=0, bytes_accessed=2 << 20, transcendentals=0),
    )(slots, core, video, text)
    got = swap(give)
    valid_other = swap(text_valid)
    buf = pl.pallas_call(
        pack_kernel, out_shape=shape(SEQ, 3, ROWS, HD), in_specs=[SMEM, SMEM, ANY, ANY],
        out_specs=VMEM, scratch_shapes=[pltpu.SemaphoreType.DMA((4,))], name="pack",
        cost_estimate=pl.CostEstimate(flops=0, bytes_accessed=7 << 20, transcendentals=0),
    )(slots, core, video, text)
    buf = pl.pallas_call(
        fill_kernel, out_shape=shape(SEQ, 3, ROWS, HD), in_specs=[SMEM, VMEM, ANY],
        out_specs=ANY, scratch_shapes=[pltpu.SemaphoreType.DMA((1,))], name="fill",
        input_output_aliases={2: 0},
    )(core, got, buf)
    buf, weight, cot = lax.optimization_barrier((buf, text_weight, text_cotangent[0]))
    weight_x = gather4(weight, "seq", 1).reshape(4 * 256, 384)
    cot = by_xor(cot.reshape(TT, 8, 384).transpose(1, 0, 2), dp)
    cot = gather4(exchange_dp(cot).reshape(8 * TT, 384), "seq", 4)
    cot_y = cot.reshape(4, 8, TT, 384).transpose(1, 0, 2, 3).reshape(8 * 4 * TT, 384)
    recv = lax.all_to_all(buf, "seq", split_axis=0, concat_axis=0, tiled=True)
    other = swap(recv[:, 1:3, VT + TT:VT + TT + HALF, :])

    bias_a = jnp.where(text_valid > 0, 0.0, -1e30).astype(F32)
    bias_far = jnp.where(valid_other > 0, 0.0, -1e30).astype(F32)
    bias_c = jnp.where(seq % 2 == core_bit, bias_a, bias_far)

    text_out = attention_call(
        text_kernel, "text_attention", 2 * TXT, TXT, 2, shape(SEQ, 2 * TT, HD), [VMEM] * 4 + [ANY] * 2,
    )(bias_a, bias_c, recv, other, weight_x, cot_y)
    text_got = lax.all_to_all(text_out, "seq", split_axis=0, concat_axis=0, tiled=True)
    out_a = attention_call(
        a_kernel, "video_attention_a", VID, 2 * VT, 1, shape(SEQ, VT, HD), [VMEM] * 2,
    )(bias_a, recv)
    out_all = attention_call(
        c_kernel, "video_attention_c", VID // 2, 4 * HALF, 1, shape(SEQ, VT + HALF, HD), [VMEM] * 4,
    )(bias_c, recv, other, out_a)
    back = lax.all_to_all(out_all, "seq", split_axis=0, concat_axis=0, tiled=True)
    halves = back.reshape(8, 2, VT + HALF, HD)[:, :, VT:, :]
    halves = swap(lax.dynamic_index_in_dim(halves, 1 - core_bit, 1, keepdims=False))
    video_attended = pl.pallas_call(
        slot_video_kernel, out_shape=shape(VT, SLOTS * HD), in_specs=[SMEM, SMEM, VMEM, VMEM],
        out_specs=VMEM, name="slot_video")(ranks, core, back, halves)

    text_slots = pl.pallas_call(
        slot_text_kernel, out_shape=shape(4, TT, 8 * HD),
        in_specs=[SMEM, SMEM, SMEM, VMEM, ANY], out_specs=VMEM, name="slot_text",
    )(ranks, core, seat, text_got, out_all)
    rows = [text_slots[0]] + [trade(text_slots[j], "seq", 4 * j) for j in (1, 2, 3)]
    rows_all = gather_dp(jnp.concatenate(rows)).reshape(8 * 4 * TT, 8 * HD)
    sums = pl.pallas_call(
        project_kernel,
        out_shape=[shape(8, TT, 384, dtype=F32)] + [shape(8, TT, 384)] * 3
        + [shape(256, 384, dtype=F32)] + [shape(256, 384)] * 3,
        in_specs=[VMEM] * 3, out_specs=[VMEM] * 8, name="project",
        compiler_params=pltpu.CompilerParams(vmem_limit_bytes=20 << 20),
    )(rows_all, weight_x, cot_y)
    projected = sums[0]
    for j in (1, 2, 3):
        projected = projected + trade(sums[j], "seq", 4 * j).astype(F32)
    gradient = sums[4]
    for j in (1, 2, 3):
        gradient = gradient + trade(sums[4 + j], "seq", j).astype(F32)
    projected = by_xor(exchange_dp(projected.astype(BF16)), dp)
    text_output = projected.transpose(1, 0, 2).reshape(TT, 8 * 384)
    return (video_attended[None], text_output[None], gradient)


def solution(mesh):
    in_specs = (
        P("dp", "seq", None, None),
        P("dp", "seq", None, None),
        P(),
        P("dp", None),
        P("seq", "dp"),
        P("dp", "seq", None),
    )
    out_specs = (P("dp", "seq", None), P("dp", "seq", None), P("seq", "dp"))
    return jax.shard_map(
        on_device, mesh=mesh, in_specs=in_specs, out_specs=out_specs, check_vma=False
    )
```

```python
import functools

import numpy as np

import jax
import jax.numpy as jnp
from jax import lax
from jax.experimental import pallas as pl
from jax.experimental.pallas import tpu as pltpu
from jax.sharding import PartitionSpec as P

HD = 128
LIVE = 24
SLOTS = 32
N = 3328
VID = 3072
TXT = 256
SEQ = 16
VT = 192
TT = 16
HALF = 96
ROWS = VT + TT + HALF + TT
CHUNK = 256
SCALE = float(np.log2(np.e) / HD**0.5)
BF16 = jnp.bfloat16
F32 = jnp.float32
VMEM = pl.BlockSpec(memory_space=pltpu.VMEM)
SMEM = pl.BlockSpec(memory_space=pltpu.SMEM)
ANY = pl.BlockSpec(memory_space=pl.ANY)


def run_all(copies):
    for copy in copies:
        copy.start()
    for copy in copies:
        copy.wait()


def list_live(live, slots):
    def body(h, counts):
        alive = live[h] > 0
        at = jnp.where(alive, counts[0], LIVE + counts[1])
        slots[jnp.clip(at, 0, SLOTS - 1)] = h
        one = jnp.where(alive, 1, 0)
        return counts[0] + one, counts[1] + 1 - one

    lax.fori_loop(0, SLOTS, body, (jnp.int32(0), jnp.int32(0)))


def head_columns(slots, rank):
    return pl.ds(pl.multiple_of(slots[rank] * HD, HD), HD)


def give_kernel(live, core, video, text, give, slots, sem):
    list_live(live, slots)
    start = pl.multiple_of((1 - core[0]) * HALF, 16)
    copies = []
    for j in range(8):
        cols = head_columns(slots, 16 + j)
        copies.append(pltpu.make_async_copy(
            video.at[:, pl.ds(start, HALF), cols], give.at[j, :, pl.ds(0, HALF), :], sem.at[0]))
        copies.append(pltpu.make_async_copy(
            text.at[:, :, cols], give.at[j, :, pl.ds(HALF, TT), :], sem.at[1]))
    run_all(copies)


def pack_kernel(live, core, video, text, buf, slots, sem):
    list_live(live, slots)
    start = pl.multiple_of(core[0] * HALF, 16)
    copies = []
    for r in range(16):
        cols = head_columns(slots, r)
        copies.append(pltpu.make_async_copy(
            video.at[:, :, cols], buf.at[r, :, pl.ds(0, VT), :], sem.at[0]))
        copies.append(pltpu.make_async_copy(
            text.at[:, :, cols], buf.at[r, :, pl.ds(VT, TT), :], sem.at[1]))
    for j in range(8):
        cols = head_columns(slots, 16 + j)
        to = 2 * j + core[0]
        copies.append(pltpu.make_async_copy(
            video.at[:, pl.ds(start, HALF), cols], buf.at[to, :, pl.ds(VT + TT, HALF), :], sem.at[2]))
        copies.append(pltpu.make_async_copy(
            text.at[:, :, cols], buf.at[to, :, pl.ds(VT + TT + HALF, TT), :], sem.at[3]))
    run_all(copies)


def fill_kernel(core, got, _, buf, sem):
    copies = []
    for j in range(8):
        to = 2 * j + 1 - core[0]
        copies.append(pltpu.make_async_copy(
            got.at[j], buf.at[to, :, pl.ds(VT + TT, HALF + TT), :], sem))
    run_all(copies)


def rows_dot(a, b):
    return lax.dot_general(a, b, (((1,), (1,)), ((), ())), preferred_element_type=F32)


def lay_a(recv, keys, values):
    for s in range(SEQ):
        keys[s * VT:(s + 1) * VT, :] = recv[s, 1, 0:VT, :]
        values[s * VT:(s + 1) * VT, 0:HD] = recv[s, 2, 0:VT, :]
        keys[VID + s * TT:VID + (s + 1) * TT, :] = recv[s, 1, VT:VT + TT, :]
        values[VID + s * TT:VID + (s + 1) * TT, 0:HD] = recv[s, 2, VT:VT + TT, :]
    values[:, HD:] = jnp.ones((N, HD), BF16)


def lay_c(recv, other, keys, values):
    first, tail = VT + TT, VT + TT + HALF
    for s in range(SEQ):
        at, far = s * HALF, VID // 2 + s * HALF
        keys[at:at + HALF, :] = recv[s, 1, first:tail, :]
        values[at:at + HALF, 0:HD] = recv[s, 2, first:tail, :]
        keys[far:far + HALF, :] = other[s, 0]
        values[far:far + HALF, 0:HD] = other[s, 1]
        keys[VID + s * TT:VID + (s + 1) * TT, :] = recv[s, 1, tail:ROWS, :]
        values[VID + s * TT:VID + (s + 1) * TT, 0:HD] = recv[s, 2, tail:ROWS, :]
    values[:, HD:] = jnp.ones((N, HD), BF16)


def score_chunk(query, keys, bias, scores, slot, c, top):
    rows = query.shape[0]
    s = rows_dot(query, keys[c:c + CHUNK, :])
    if c >= VID:
        s = s + bias[:, c - VID:c - VID + CHUNK]
    scores[slot, 0:rows, c:c + CHUNK] = s
    for t in range(0, CHUNK, HD):
        x = s[:, t:t + HD]
        top = x if top is None else jnp.maximum(top, x)
    return top


def keep_top(tops, slot, top):
    rows = top.shape[0]
    highest = jnp.max(top, axis=1, keepdims=True) * SCALE
    tops[slot, 0:rows, :] = jnp.broadcast_to(highest, (rows, HD))


def score_block(query, keys, bias, scores, tops, slot):
    top = None
    for c in range(0, N, CHUNK):
        top = score_chunk(query, keys, bias, scores, slot, c, top)
    keep_top(tops, slot, top)


def attend_block(rows, values, scores, tops, slot, following=None):
    highest = jnp.concatenate([tops[slot, 0:rows, :]] * (CHUNK // HD), axis=1)
    top, total = None, None
    for c in range(0, N, CHUNK):
        if following is not None:
            query, keys, bias = following
            top = score_chunk(query, keys, bias, scores, 1 - slot, c, top)
        p = jnp.exp2(scores[slot, 0:rows, c:c + CHUNK] * SCALE - highest)
        part = jnp.dot(p.astype(BF16), values[c:c + CHUNK, :], preferred_element_type=F32)
        total = part if total is None else total + part
    if following is not None:
        keep_top(tops, 1 - slot, top)
    return (total[:, 0:HD] / total[:, HD:]).astype(BF16)


def put_text(out, at, got):
    got = got.reshape(4, 4, TT, HD)
    for s in range(SEQ):
        for y in range(4):
            out[s, at + y * TT:at + (y + 1) * TT, :] = got[y, s % 4]


def text_kernel(bias_a, bias_c, recv, other, out, token, scores, tops, keys_a, values_a, keys_c, values_c):
    lay_a(recv, keys_a, values_a)
    ba, bc = bias_a[...], bias_c[...]
    score_block(recv[:, 0, VT:VT + TT, :].reshape(TXT, HD), keys_a, ba, scores, tops, 0)
    lay_c(recv, other, keys_c, values_c)
    query = recv[:, 0, VT + TT + HALF:ROWS, :].reshape(TXT, HD)
    got = attend_block(TXT, values_a, scores, tops, 0, (query, keys_c, bc))
    put_text(out, 0, got)
    put_text(out, 4 * TT, attend_block(TXT, values_c, scores, tops, 1))
    token[...] = jnp.zeros_like(token)


def video_blocks(count, rows, load, store, keys, values, bias, scores, tops):
    def step(i, slot, more):
        following = (load(i + 1), keys, bias) if more else None
        store(i, attend_block(rows, values, scores, tops, slot, following))

    score_block(load(0), keys, bias, scores, tops, 0)

    def body(j, carry):
        step(2 * j, 0, True)
        step(2 * j + 1, 1, True)
        return carry

    lax.fori_loop(0, count // 2 - 1, body, 0)
    step(count - 2, 0, True)
    step(count - 1, 1, False)


def a_kernel(bias_a, recv, _, out, token, scores, tops, keys, values):
    lay_a(recv, keys, values)

    def load(i):
        return recv[pl.ds(2 * i, 2), 0, 0:VT, :].reshape(2 * VT, HD)

    def store(i, got):
        out[pl.ds(2 * i, 2)] = got.reshape(2, VT, HD)

    video_blocks(8, 2 * VT, load, store, keys, values, bias_a[...], scores, tops)
    token[...] = jnp.zeros_like(token)


def c_kernel(bias_c, recv, other, out_a, _, out, token, scores, tops, keys, values):
    out[:, 0:VT, :] = out_a[...]
    token[...] = jnp.zeros_like(token)
    lay_c(recv, other, keys, values)

    def load(i):
        return recv[pl.ds(4 * i, 4), 0, VT + TT:VT + TT + HALF, :].reshape(4 * HALF, HD)

    def store(i, got):
        out[pl.ds(4 * i, 4), VT:, :] = got.reshape(4, HALF, HD)

    video_blocks(4, 4 * HALF, load, store, keys, values, bias_c[...], scores, tops)


def slot_text_kernel(ranks, core, seat, got, _t, _w, _c, out, token):
    token[...] = jnp.zeros_like(token)
    y, x = seat[0] // 4, seat[0] % 4
    for k in range(8):
        rank = ranks[8 * y + k]
        cols = pl.ds(pl.multiple_of((((k // 2) ^ x) * 2 + k % 2) * HD, HD), HD)
        source = jnp.where(rank < 16, jnp.clip(rank, 0, 15), 2 * jnp.clip(rank - 16, 0, 7) + core[0])
        base = jnp.where(rank < 16, 0, 4 * TT)
        for j in range(4):
            block = got[source, pl.ds(pl.multiple_of(base + (j ^ y) * TT, TT), TT), :]
            out[j * TT:(j + 1) * TT, cols] = jnp.where(rank >= 0, block, jnp.zeros_like(block))


def project_kernel(rows, weight, cot, p0, p1, p2, p3, g0, g1, g2, g3):
    part = jnp.dot(rows[...], weight[...], preferred_element_type=F32).reshape(8, 4, TT, 384)
    for j, ref in enumerate((p0, p1, p2, p3)):
        ref[...] = part[:, j].astype(ref.dtype)
    for j, ref in enumerate((g0, g1, g2, g3)):
        term = lax.dot_general(
            rows[:, j * 256:(j + 1) * 256], cot[...], (((0,), (0,)), ((), ())),
            preferred_element_type=F32)
        ref[...] = term.astype(ref.dtype)


def slot_video_kernel(live, core, got, other, out, slots):
    list_live(live, slots)
    mine = pl.multiple_of(core[0] * HALF, 16)
    far = pl.multiple_of((1 - core[0]) * HALF, 16)
    for r in range(16):
        out[:, head_columns(slots, r)] = got[r, 0:VT, :]
    for j in range(8):
        cols = head_columns(slots, 16 + j)
        out[pl.ds(mine, HALF), cols] = got[2 * j + core[0], VT:, :]
        out[pl.ds(far, HALF), cols] = other[j]
        out[:, head_columns(slots, LIVE + j)] = jnp.zeros((VT, HD), BF16)


def shape(*dims, dtype=BF16):
    return jax.ShapeDtypeStruct(dims, dtype)


def cost(rows):
    return pl.CostEstimate(
        flops=4 * rows * N * HD, bytes_accessed=8 << 20, transcendentals=rows * N)


def attention_call(kernel, name, rows, block, heads, out_shape, specs):
    scratch = [pltpu.VMEM((2, block, N), F32), pltpu.VMEM((2, block, HD), F32)]
    for _ in range(heads):
        scratch += [pltpu.VMEM((N, HD), BF16), pltpu.VMEM((N, 2 * HD), BF16)]
    return pl.pallas_call(
        kernel, out_shape=[out_shape, shape(8, HD, dtype=F32)], in_specs=specs,
        out_specs=[VMEM, VMEM], scratch_shapes=scratch,
        cost_estimate=cost(rows), name=name,
        compiler_params=pltpu.CompilerParams(vmem_limit_bytes=22 << 20))


def trade(x, axis, mask):
    count = 8 if axis == "dp" else SEQ
    return lax.ppermute(x, axis, [(i, i ^ mask) for i in range(count)])


def swap(x):
    return trade(x, "dp", 1)


def by_xor(x, index):
    count, rest = x.shape[0], x.shape[1:]
    bits = count.bit_length() - 1
    for b in range(bits):
        parts = x.reshape((count >> (b + 1), 2, 1 << b) + rest)
        x = jnp.where((index >> b) & 1 > 0, parts[:, ::-1], parts).reshape((count,) + rest)
    return x


def direct4(x, axis, low):
    return jnp.stack([x] + [trade(x, axis, j * low) for j in (1, 2, 3)])


def exchange_round(x, b):
    rest = x.shape[1:]
    parts = x.reshape((8 >> (b + 1), 2, 1 << b) + rest)
    got = trade(parts[:, 1], "dp", 1 << b)
    return jnp.stack([parts[:, 0], got], axis=1).reshape((8,) + rest)


def exchange_dp(x):
    for b in (2, 1, 0):
        x = exchange_round(x, b)
    return x


def on_device(video_projected, text_projected, head_live, text_valid, text_weight, text_cotangent):
    video = video_projected[0].transpose(1, 0, 2)
    text = text_projected[0].transpose(1, 0, 2)
    seq = lax.axis_index("seq")
    dp = lax.axis_index("dp")
    core_bit = dp % 2
    core = core_bit.astype(jnp.int32).reshape(1)
    seat = seq.astype(jnp.int32).reshape(1)

    heads = jnp.arange(SLOTS, dtype=jnp.int32)
    before = jnp.sum(jnp.where(heads[None, :] < heads[:, None], head_live[None, :], 0), axis=1)
    ranks = jnp.where(head_live > 0, before, -1).astype(jnp.int32)

    slots_scratch = pltpu.SMEM((SLOTS,), jnp.int32)
    give = pl.pallas_call(
        give_kernel, out_shape=shape(8, 3, HALF + TT, HD), in_specs=[SMEM, SMEM, ANY, ANY],
        out_specs=VMEM, scratch_shapes=[slots_scratch, pltpu.SemaphoreType.DMA((2,))], name="give",
        cost_estimate=pl.CostEstimate(flops=0, bytes_accessed=2 << 20, transcendentals=0),
    )(head_live, core, video, text)
    got = swap(give)
    valid_other = swap(text_valid)
    buf = pl.pallas_call(
        pack_kernel, out_shape=shape(SEQ, 3, ROWS, HD), in_specs=[SMEM, SMEM, ANY, ANY],
        out_specs=VMEM, scratch_shapes=[slots_scratch, pltpu.SemaphoreType.DMA((4,))], name="pack",
        cost_estimate=pl.CostEstimate(flops=0, bytes_accessed=7 << 20, transcendentals=0),
    )(head_live, core, video, text)
    buf = pl.pallas_call(
        fill_kernel, out_shape=shape(SEQ, 3, ROWS, HD), in_specs=[SMEM, VMEM, ANY],
        out_specs=ANY, scratch_shapes=[pltpu.SemaphoreType.DMA], name="fill",
        input_output_aliases={2: 0},
    )(core, got, buf)
    cot = by_xor(text_cotangent[0].reshape(TT, 8, 384).transpose(1, 0, 2), dp)
    cot = exchange_dp(cot).reshape(8 * TT, 384)
    buf, valid_other, cot = lax.optimization_barrier((buf, valid_other, cot))
    recv = lax.all_to_all(buf, "seq", split_axis=0, concat_axis=0, tiled=True)
    other = swap(recv[:, 1:3, VT + TT:VT + TT + HALF, :])

    bias_a = jnp.where(text_valid > 0, 0.0, -1e30).astype(F32)
    bias_far = jnp.where(valid_other > 0, 0.0, -1e30).astype(F32)
    bias_c = jnp.where(seq % 2 == core_bit, bias_a, bias_far)

    text_out, token = attention_call(
        text_kernel, "text_attention", 2 * TXT, TXT, 2, shape(SEQ, 8 * TT, HD), [VMEM] * 4,
    )(bias_a, bias_c, recv, other)
    text_out, weight, cot = lax.optimization_barrier((text_out, text_weight, cot))
    weight_x = direct4(weight, "seq", 1).reshape(4 * 256, 384)
    cot = direct4(cot, "seq", 4)
    cot_y = cot.reshape(4, 8, TT, 384).transpose(1, 0, 2, 3).reshape(8 * 4 * TT, 384)
    text_got = lax.all_to_all(text_out, "seq", split_axis=0, concat_axis=0, tiled=True)

    out_a, token = attention_call(
        a_kernel, "video_attention_a", VID, 2 * VT, 1, shape(SEQ, VT, HD), [VMEM] * 3,
    )(bias_a, recv, token)
    text_rows, token = pl.pallas_call(
        slot_text_kernel, out_shape=[shape(4 * TT, 8 * HD), shape(8, HD, dtype=F32)],
        in_specs=[SMEM, SMEM, SMEM, VMEM, VMEM, ANY, ANY], out_specs=[VMEM, VMEM],
        name="slot_text",
    )(ranks, core, seat, text_got, token, weight_x, cot_y)
    out_c, _ = attention_call(
        c_kernel, "video_attention_c", VID // 2, 4 * HALF, 1, shape(SEQ, VT + HALF, HD),
        [VMEM] * 5,
    )(bias_c, recv, other, out_a, token)
    rows_near = direct4(text_rows, "dp", 2)
    out_c, rows_near = lax.optimization_barrier((out_c, rows_near))
    back = lax.all_to_all(out_c, "seq", split_axis=0, concat_axis=0, tiled=True)
    rows_far = swap(rows_near)
    rows_all = jnp.stack([rows_near, rows_far], axis=1).reshape(8 * 4 * TT, 8 * HD)
    sums = pl.pallas_call(
        project_kernel,
        out_shape=[shape(8, TT, 384, dtype=F32)] + [shape(8, TT, 384)] * 3
        + [shape(256, 384, dtype=F32)] + [shape(256, 384)] * 3,
        in_specs=[VMEM] * 3, out_specs=[VMEM] * 8, name="project",
        compiler_params=pltpu.CompilerParams(vmem_limit_bytes=20 << 20),
    )(rows_all, weight_x, cot_y)
    projected = sums[0]
    for j in (1, 2, 3):
        projected = projected + trade(sums[j], "seq", 4 * j).astype(F32)
    gradient = sums[4]
    for j in (1, 2, 3):
        gradient = gradient + trade(sums[4 + j], "seq", j).astype(F32)
    projected, back = lax.optimization_barrier((projected.astype(BF16), back))
    halves = swap(lax.dynamic_index_in_dim(
        back.reshape(8, 2, VT + HALF, HD)[:, :, VT:], 1 - core_bit, 1, keepdims=False))
    video_attended = pl.pallas_call(
        slot_video_kernel, out_shape=shape(VT, SLOTS * HD), in_specs=[SMEM, SMEM] + [VMEM] * 2,
        out_specs=VMEM, scratch_shapes=[slots_scratch], name="slot_video",
    )(head_live, core, back, halves)

    projected = by_xor(exchange_dp(projected), dp)
    text_output = projected.transpose(1, 0, 2).reshape(TT, 8 * 384)
    return (video_attended[None], text_output[None], gradient)


def solution(mesh):
    in_specs = (
        P("dp", "seq", None, None),
        P("dp", "seq", None, None),
        P(),
        P("dp", None),
        P("seq", "dp"),
        P("dp", "seq", None),
    )
    out_specs = (P("dp", "seq", None), P("dp", "seq", None), P("seq", "dp"))
    return jax.shard_map(
        on_device, mesh=mesh, in_specs=in_specs, out_specs=out_specs, check_vma=False
    )
```

```python
import functools

import numpy as np

import jax
import jax.numpy as jnp
from jax import lax
from jax.experimental import pallas as pl
from jax.experimental.pallas import tpu as pltpu
from jax.sharding import PartitionSpec as P

HD = 128
LIVE = 24
SLOTS = 32
N = 3328
VID = 3072
TXT = 256
SEQ = 16
VT = 192
TT = 16
HALF = 96
ROWS = VT + TT + HALF + TT
CHUNK = 256
SCALE = float(np.log2(np.e) / HD**0.5)
BF16 = jnp.bfloat16
F32 = jnp.float32
VMEM = pl.BlockSpec(memory_space=pltpu.VMEM)
SMEM = pl.BlockSpec(memory_space=pltpu.SMEM)
ANY = pl.BlockSpec(memory_space=pl.ANY)


def run_all(copies):
    for copy in copies:
        copy.start()
    for copy in copies:
        copy.wait()


def list_live(live, slots):
    def body(h, counts):
        alive = live[h] > 0
        at = jnp.where(alive, counts[0], LIVE + counts[1])
        slots[jnp.clip(at, 0, SLOTS - 1)] = h
        one = jnp.where(alive, 1, 0)
        return counts[0] + one, counts[1] + 1 - one

    lax.fori_loop(0, SLOTS, body, (jnp.int32(0), jnp.int32(0)))


def head_columns(slots, rank):
    return pl.ds(pl.multiple_of(slots[rank] * HD, HD), HD)


def give_kernel(live, core, video, text, give, slots, sem):
    list_live(live, slots)
    start = pl.multiple_of((1 - core[0]) * HALF, 16)
    copies = []
    for j in range(8):
        cols = head_columns(slots, 16 + j)
        copies.append(pltpu.make_async_copy(
            video.at[:, pl.ds(start, HALF), cols], give.at[j, :, pl.ds(0, HALF), :], sem.at[0]))
        copies.append(pltpu.make_async_copy(
            text.at[:, :, cols], give.at[j, :, pl.ds(HALF, TT), :], sem.at[1]))
    run_all(copies)


def pack_kernel(live, core, video, text, buf, slots, sem):
    list_live(live, slots)
    start = pl.multiple_of(core[0] * HALF, 16)
    copies = []
    for r in range(16):
        cols = head_columns(slots, r)
        copies.append(pltpu.make_async_copy(
            video.at[:, :, cols], buf.at[r, :, pl.ds(0, VT), :], sem.at[0]))
        copies.append(pltpu.make_async_copy(
            text.at[:, :, cols], buf.at[r, :, pl.ds(VT, TT), :], sem.at[1]))
    for j in range(8):
        cols = head_columns(slots, 16 + j)
        to = 2 * j + core[0]
        copies.append(pltpu.make_async_copy(
            video.at[:, pl.ds(start, HALF), cols], buf.at[to, :, pl.ds(VT + TT, HALF), :], sem.at[2]))
        copies.append(pltpu.make_async_copy(
            text.at[:, :, cols], buf.at[to, :, pl.ds(VT + TT + HALF, TT), :], sem.at[3]))
    run_all(copies)


def fill_kernel(core, got, _, buf, sem):
    copies = []
    for j in range(8):
        to = 2 * j + 1 - core[0]
        copies.append(pltpu.make_async_copy(
            got.at[j], buf.at[to, :, pl.ds(VT + TT, HALF + TT), :], sem))
    run_all(copies)


def rows_dot(a, b):
    return lax.dot_general(a, b, (((1,), (1,)), ((), ())), preferred_element_type=F32)


def lay_a(recv, keys, values):
    for s in range(SEQ):
        keys[s * VT:(s + 1) * VT, :] = recv[s, 1, 0:VT, :]
        values[s * VT:(s + 1) * VT, 0:HD] = recv[s, 2, 0:VT, :]
        keys[VID + s * TT:VID + (s + 1) * TT, :] = recv[s, 1, VT:VT + TT, :]
        values[VID + s * TT:VID + (s + 1) * TT, 0:HD] = recv[s, 2, VT:VT + TT, :]
    values[:, HD:] = jnp.ones((N, HD), BF16)


def lay_c(recv, other, keys, values):
    first, tail = VT + TT, VT + TT + HALF
    for s in range(SEQ):
        at, far = s * HALF, VID // 2 + s * HALF
        keys[at:at + HALF, :] = recv[s, 1, first:tail, :]
        values[at:at + HALF, 0:HD] = recv[s, 2, first:tail, :]
        keys[far:far + HALF, :] = other[s, 0]
        values[far:far + HALF, 0:HD] = other[s, 1]
        keys[VID + s * TT:VID + (s + 1) * TT, :] = recv[s, 1, tail:ROWS, :]
        values[VID + s * TT:VID + (s + 1) * TT, 0:HD] = recv[s, 2, tail:ROWS, :]
    values[:, HD:] = jnp.ones((N, HD), BF16)


def score_chunk(query, keys, bias, scores, slot, c, top):
    rows = query.shape[0]
    s = rows_dot(query, keys[c:c + CHUNK, :])
    if c >= VID:
        s = s + bias[:, c - VID:c - VID + CHUNK]
    scores[slot, 0:rows, c:c + CHUNK] = s
    for t in range(0, CHUNK, HD):
        x = s[:, t:t + HD]
        top = x if top is None else jnp.maximum(top, x)
    return top


def keep_top(tops, slot, top):
    rows = top.shape[0]
    highest = jnp.max(top, axis=1, keepdims=True) * SCALE
    tops[slot, 0:rows, :] = jnp.broadcast_to(highest, (rows, HD))


def score_block(query, keys, bias, scores, tops, slot):
    top = None
    for c in range(0, N, CHUNK):
        top = score_chunk(query, keys, bias, scores, slot, c, top)
    keep_top(tops, slot, top)


def attend_block(rows, values, scores, tops, slot, following=None):
    highest = jnp.concatenate([tops[slot, 0:rows, :]] * (CHUNK // HD), axis=1)
    top, total = None, None
    for c in range(0, N, CHUNK):
        if following is not None:
            query, keys, bias = following
            top = score_chunk(query, keys, bias, scores, 1 - slot, c, top)
        p = jnp.exp2(scores[slot, 0:rows, c:c + CHUNK] * SCALE - highest)
        part = jnp.dot(p.astype(BF16), values[c:c + CHUNK, :], preferred_element_type=F32)
        total = part if total is None else total + part
    if following is not None:
        keep_top(tops, 1 - slot, top)
    return (total[:, 0:HD] / total[:, HD:]).astype(BF16)


def put_text(out, at, got):
    got = got.reshape(4, 4, TT, HD)
    for s in range(SEQ):
        for y in range(4):
            out[s, at + y * TT:at + (y + 1) * TT, :] = got[y, s % 4]


def text_kernel(bias_a, bias_c, recv, other, out, token, scores, tops, keys_a, values_a, keys_c, values_c):
    lay_a(recv, keys_a, values_a)
    ba, bc = bias_a[...], bias_c[...]
    score_block(recv[:, 0, VT:VT + TT, :].reshape(TXT, HD), keys_a, ba, scores, tops, 0)
    lay_c(recv, other, keys_c, values_c)
    query = recv[:, 0, VT + TT + HALF:ROWS, :].reshape(TXT, HD)
    got = attend_block(TXT, values_a, scores, tops, 0, (query, keys_c, bc))
    put_text(out, 0, got)
    put_text(out, 4 * TT, attend_block(TXT, values_c, scores, tops, 1))
    token[...] = jnp.zeros_like(token)


def video_blocks(count, rows, load, store, keys, values, bias, scores, tops):
    def step(i, slot, more):
        following = (load(i + 1), keys, bias) if more else None
        store(i, attend_block(rows, values, scores, tops, slot, following))

    score_block(load(0), keys, bias, scores, tops, 0)

    def body(j, carry):
        step(2 * j, 0, True)
        step(2 * j + 1, 1, True)
        return carry

    lax.fori_loop(0, count // 2 - 1, body, 0)
    step(count - 2, 0, True)
    step(count - 1, 1, False)


def a_kernel(bias_a, recv, _, out, token, scores, tops, keys, values):
    lay_a(recv, keys, values)

    def load(i):
        return recv[pl.ds(2 * i, 2), 0, 0:VT, :].reshape(2 * VT, HD)

    def store(i, got):
        out[pl.ds(2 * i, 2)] = got.reshape(2, VT, HD)

    video_blocks(8, 2 * VT, load, store, keys, values, bias_a[...], scores, tops)
    token[...] = jnp.zeros_like(token)


def c_kernel(bias_c, recv, other, out_a, _, out, token, scores, tops, keys, values):
    out[:, 0:VT, :] = out_a[...]
    token[...] = jnp.zeros_like(token)
    lay_c(recv, other, keys, values)

    def load(i):
        return recv[pl.ds(4 * i, 4), 0, VT + TT:VT + TT + HALF, :].reshape(4 * HALF, HD)

    def store(i, got):
        out[pl.ds(4 * i, 4), VT:, :] = got.reshape(4, HALF, HD)

    video_blocks(4, 4 * HALF, load, store, keys, values, bias_c[...], scores, tops)


def list_ranks(live, ranks):
    def body(h, count):
        alive = live[h] > 0
        ranks[h] = jnp.where(alive, count, -1)
        return count + jnp.where(alive, 1, 0)

    lax.fori_loop(0, SLOTS, body, jnp.int32(0))


def slot_text_kernel(live, core, seat, got, *rest):
    out, token, ranks = rest[-3:]
    token[...] = jnp.zeros_like(token)
    list_ranks(live, ranks)
    y, x = seat[0] // 4, seat[0] % 4
    for k in range(8):
        rank = ranks[8 * y + k]
        cols = pl.ds(pl.multiple_of((((k // 2) ^ x) * 2 + k % 2) * HD, HD), HD)
        source = jnp.where(rank < 16, jnp.clip(rank, 0, 15), 2 * jnp.clip(rank - 16, 0, 7) + core[0])
        base = jnp.where(rank < 16, 0, 4 * TT)
        for j in range(4):
            block = got[source, pl.ds(pl.multiple_of(base + (j ^ y) * TT, TT), TT), :]
            out[j * TT:(j + 1) * TT, cols] = jnp.where(rank >= 0, block, jnp.zeros_like(block))


def project_kernel(near, far, w0, w1, w2, w3, c0, c1, c2, c3, p0, p1, p2, p3, g0, g1, g2, g3, rows, cot):
    for z in range(4):
        rows[z * 128:z * 128 + 64, :] = near[z]
        rows[z * 128 + 64:(z + 1) * 128, :] = far[z]
    for w in range(8):
        for j, ref in enumerate((c0, c1, c2, c3)):
            at = (w * 4 + j) * TT
            cot[at:at + TT, :] = ref[w * TT:(w + 1) * TT, :]
    part = None
    for j, ref in enumerate((w0, w1, w2, w3)):
        term = jnp.dot(rows[:, j * 256:(j + 1) * 256], ref[...], preferred_element_type=F32)
        part = term if part is None else part + term
    part = part.reshape(8, 4, TT, 384)
    for j, ref in enumerate((p0, p1, p2, p3)):
        ref[...] = part[:, j].astype(ref.dtype)
    for j, ref in enumerate((g0, g1, g2, g3)):
        term = lax.dot_general(
            rows[:, j * 256:(j + 1) * 256], cot[...], (((0,), (0,)), ((), ())),
            preferred_element_type=F32)
        ref[...] = term.astype(ref.dtype)


def slot_video_kernel(live, core, got, other, out, slots):
    list_live(live, slots)
    mine = pl.multiple_of(core[0] * HALF, 16)
    far = pl.multiple_of((1 - core[0]) * HALF, 16)
    for r in range(16):
        out[:, head_columns(slots, r)] = got[r, 0:VT, :]
    for j in range(8):
        cols = head_columns(slots, 16 + j)
        out[pl.ds(mine, HALF), cols] = got[2 * j + core[0], VT:, :]
        out[pl.ds(far, HALF), cols] = other[j]
        out[:, head_columns(slots, LIVE + j)] = jnp.zeros((VT, HD), BF16)


def shape(*dims, dtype=BF16):
    return jax.ShapeDtypeStruct(dims, dtype)


def cost(rows):
    return pl.CostEstimate(
        flops=4 * rows * N * HD, bytes_accessed=8 << 20, transcendentals=rows * N)


def attention_call(kernel, name, rows, block, heads, out_shape, specs):
    scratch = [pltpu.VMEM((2, block, N), F32), pltpu.VMEM((2, block, HD), F32)]
    for _ in range(heads):
        scratch += [pltpu.VMEM((N, HD), BF16), pltpu.VMEM((N, 2 * HD), BF16)]
    return pl.pallas_call(
        kernel, out_shape=[out_shape, shape(8, HD, dtype=F32)], in_specs=specs,
        out_specs=[VMEM, VMEM], scratch_shapes=scratch,
        cost_estimate=cost(rows), name=name,
        compiler_params=pltpu.CompilerParams(vmem_limit_bytes=22 << 20))


def trade(x, axis, mask):
    count = 8 if axis == "dp" else SEQ
    return lax.ppermute(x, axis, [(i, i ^ mask) for i in range(count)])


def swap(x):
    return trade(x, "dp", 1)


def by_xor(x, index):
    count, rest = x.shape[0], x.shape[1:]
    bits = count.bit_length() - 1
    for b in range(bits):
        parts = x.reshape((count >> (b + 1), 2, 1 << b) + rest)
        x = jnp.where((index >> b) & 1 > 0, parts[:, ::-1], parts).reshape((count,) + rest)
    return x


def direct4(x, axis, low):
    return [x] + [trade(x, axis, j * low) for j in (1, 2, 3)]


def exchange_round(x, b):
    rest = x.shape[1:]
    parts = x.reshape((8 >> (b + 1), 2, 1 << b) + rest)
    got = trade(parts[:, 1], "dp", 1 << b)
    return jnp.stack([parts[:, 0], got], axis=1).reshape((8,) + rest)


def on_device(video_projected, text_projected, head_live, text_valid, text_weight, text_cotangent):
    video = video_projected[0].transpose(1, 0, 2)
    text = text_projected[0].transpose(1, 0, 2)
    seq = lax.axis_index("seq")
    dp = lax.axis_index("dp")
    core_bit = dp % 2
    core = core_bit.astype(jnp.int32).reshape(1)
    seat = seq.astype(jnp.int32).reshape(1)

    slots_scratch = pltpu.SMEM((SLOTS,), jnp.int32)
    give = pl.pallas_call(
        give_kernel, out_shape=shape(8, 3, HALF + TT, HD), in_specs=[SMEM, SMEM, ANY, ANY],
        out_specs=VMEM, scratch_shapes=[slots_scratch, pltpu.SemaphoreType.DMA((2,))], name="give",
        cost_estimate=pl.CostEstimate(flops=0, bytes_accessed=2 << 20, transcendentals=0),
    )(head_live, core, video, text)
    got = swap(give)
    valid_other = swap(text_valid)
    buf = pl.pallas_call(
        pack_kernel, out_shape=shape(SEQ, 3, ROWS, HD), in_specs=[SMEM, SMEM, ANY, ANY],
        out_specs=VMEM, scratch_shapes=[slots_scratch, pltpu.SemaphoreType.DMA((4,))], name="pack",
        cost_estimate=pl.CostEstimate(flops=0, bytes_accessed=7 << 20, transcendentals=0),
    )(head_live, core, video, text)
    cot = by_xor(text_cotangent[0].reshape(TT, 8, 384).transpose(1, 0, 2), dp)
    cot = exchange_round(exchange_round(cot, 2), 1)
    buf, cot = lax.optimization_barrier((buf, cot))
    cot = exchange_round(cot, 0).reshape(8 * TT, 384)
    buf = pl.pallas_call(
        fill_kernel, out_shape=shape(SEQ, 3, ROWS, HD), in_specs=[SMEM, VMEM, ANY],
        out_specs=ANY, scratch_shapes=[pltpu.SemaphoreType.DMA], name="fill",
        input_output_aliases={2: 0},
    )(core, got, buf)
    buf, valid_other, cot = lax.optimization_barrier((buf, valid_other, cot))
    recv = lax.all_to_all(buf, "seq", split_axis=0, concat_axis=0, tiled=True)
    other = swap(recv[:, 1:3, VT + TT:VT + TT + HALF, :])

    bias_a = jnp.where(text_valid > 0, 0.0, -1e30).astype(F32)
    bias_far = jnp.where(valid_other > 0, 0.0, -1e30).astype(F32)
    bias_c = jnp.where(seq % 2 == core_bit, bias_a, bias_far)

    text_out, token = attention_call(
        text_kernel, "text_attention", 2 * TXT, TXT, 2, shape(SEQ, 8 * TT, HD), [VMEM] * 4,
    )(bias_a, bias_c, recv, other)
    text_out, weight, cot = lax.optimization_barrier((text_out, text_weight, cot))
    weight_x = direct4(weight, "seq", 1)
    cot_y = direct4(cot, "seq", 4)
    text_got = lax.all_to_all(text_out, "seq", split_axis=0, concat_axis=0, tiled=True)

    out_a, token = attention_call(
        a_kernel, "video_attention_a", VID, 2 * VT, 1, shape(SEQ, VT, HD), [VMEM] * 3,
    )(bias_a, recv, token)
    text_rows, token = pl.pallas_call(
        slot_text_kernel, out_shape=[shape(4 * TT, 8 * HD), shape(8, HD, dtype=F32)],
        in_specs=[SMEM, SMEM, SMEM, VMEM, VMEM] + [ANY] * 6, out_specs=[VMEM, VMEM],
        scratch_shapes=[slots_scratch],
        name="slot_text",
    )(head_live, core, seat, text_got, token, *weight_x[1:], *cot_y[1:])
    out_c, _ = attention_call(
        c_kernel, "video_attention_c", VID // 2, 4 * HALF, 1, shape(SEQ, VT + HALF, HD),
        [VMEM] * 5,
    )(bias_c, recv, other, out_a, token)
    rows_near = jnp.stack(direct4(text_rows, "dp", 2))
    out_c, rows_near = lax.optimization_barrier((out_c, rows_near))
    back = lax.all_to_all(out_c, "seq", split_axis=0, concat_axis=0, tiled=True)
    rows_far = swap(rows_near)
    sums = pl.pallas_call(
        project_kernel,
        out_shape=[shape(8, TT, 384, dtype=F32)] + [shape(8, TT, 384)] * 3
        + [shape(256, 384, dtype=F32)] + [shape(256, 384)] * 3,
        in_specs=[VMEM] * 10, out_specs=[VMEM] * 8, name="project",
        scratch_shapes=[pltpu.VMEM((512, 8 * HD), BF16), pltpu.VMEM((512, 384), BF16)],
        compiler_params=pltpu.CompilerParams(vmem_limit_bytes=20 << 20),
    )(rows_near, rows_far, *weight_x, *cot_y)
    projected = sums[0]
    for j in (1, 2, 3):
        projected = projected + trade(sums[j], "seq", 4 * j).astype(F32)
    gradient = sums[4]
    for j in (1, 2, 3):
        gradient = gradient + trade(sums[4 + j], "seq", j).astype(F32)
    projected, back = lax.optimization_barrier((projected.astype(BF16), back))
    halves = swap(lax.dynamic_index_in_dim(
        back.reshape(8, 2, VT + HALF, HD)[:, :, VT:], 1 - core_bit, 1, keepdims=False))
    video_attended = pl.pallas_call(
        slot_video_kernel, out_shape=shape(VT, SLOTS * HD), in_specs=[SMEM, SMEM] + [VMEM] * 2,
        out_specs=VMEM, scratch_shapes=[slots_scratch], name="slot_video",
    )(head_live, core, back, halves)

    projected = exchange_round(projected, 2)
    projected = by_xor(exchange_round(exchange_round(projected, 1), 0), dp)
    text_output = projected.transpose(1, 0, 2).reshape(TT, 8 * 384)
    return (video_attended[None], text_output[None], gradient)


def solution(mesh):
    in_specs = (
        P("dp", "seq", None, None),
        P("dp", "seq", None, None),
        P(),
        P("dp", None),
        P("seq", "dp"),
        P("dp", "seq", None),
    )
    out_specs = (P("dp", "seq", None), P("dp", "seq", None), P("seq", "dp"))
    return jax.shard_map(
        on_device, mesh=mesh, in_specs=in_specs, out_specs=out_specs, check_vma=False
    )
```

```python
import functools

import numpy as np

import jax
import jax.numpy as jnp
from jax import lax
from jax.experimental import pallas as pl
from jax.experimental.pallas import tpu as pltpu
from jax.sharding import PartitionSpec as P

HD = 128
LIVE = 24
SLOTS = 32
N = 3328
VID = 3072
TXT = 256
SEQ = 16
VT = 192
TT = 16
HALF = 96
ROWS = VT + TT + HALF + TT
CHUNK = 256
SCALE = float(np.log2(np.e) / HD**0.5)
BF16 = jnp.bfloat16
F32 = jnp.float32
VMEM = pl.BlockSpec(memory_space=pltpu.VMEM)
SMEM = pl.BlockSpec(memory_space=pltpu.SMEM)
ANY = pl.BlockSpec(memory_space=pl.ANY)


def run_all(copies):
    for copy in copies:
        copy.start()
    for copy in copies:
        copy.wait()


def list_live(live, slots):
    def body(h, counts):
        alive = live[h] > 0
        at = jnp.where(alive, counts[0], LIVE + counts[1])
        slots[jnp.clip(at, 0, SLOTS - 1)] = h
        one = jnp.where(alive, 1, 0)
        return counts[0] + one, counts[1] + 1 - one

    lax.fori_loop(0, SLOTS, body, (jnp.int32(0), jnp.int32(0)))


def head_columns(slots, rank):
    return pl.ds(pl.multiple_of(slots[rank] * HD, HD), HD)


def give_kernel(live, core, video, text, give, slots, sem):
    list_live(live, slots)
    start = pl.multiple_of((1 - core[0]) * HALF, 16)
    copies = []
    for j in range(8):
        cols = head_columns(slots, 16 + j)
        copies.append(pltpu.make_async_copy(
            video.at[:, pl.ds(start, HALF), cols], give.at[j, :, pl.ds(0, HALF), :], sem.at[0]))
        copies.append(pltpu.make_async_copy(
            text.at[:, :, cols], give.at[j, :, pl.ds(HALF, TT), :], sem.at[1]))
    run_all(copies)


def pack_kernel(live, core, video, text, buf, slots, sem):
    list_live(live, slots)
    start = pl.multiple_of(core[0] * HALF, 16)
    copies = []
    for r in range(16):
        cols = head_columns(slots, r)
        copies.append(pltpu.make_async_copy(
            video.at[:, :, cols], buf.at[r, :, pl.ds(0, VT), :], sem.at[0]))
        copies.append(pltpu.make_async_copy(
            text.at[:, :, cols], buf.at[r, :, pl.ds(VT, TT), :], sem.at[1]))
    for j in range(8):
        cols = head_columns(slots, 16 + j)
        to = 2 * j + core[0]
        copies.append(pltpu.make_async_copy(
            video.at[:, pl.ds(start, HALF), cols], buf.at[to, :, pl.ds(VT + TT, HALF), :], sem.at[2]))
        copies.append(pltpu.make_async_copy(
            text.at[:, :, cols], buf.at[to, :, pl.ds(VT + TT + HALF, TT), :], sem.at[3]))
    run_all(copies)


def fill_kernel(core, got, _, buf, sem):
    copies = []
    for j in range(8):
        to = 2 * j + 1 - core[0]
        copies.append(pltpu.make_async_copy(
            got.at[j], buf.at[to, :, pl.ds(VT + TT, HALF + TT), :], sem))
    run_all(copies)


def rows_dot(a, b):
    return lax.dot_general(a, b, (((1,), (1,)), ((), ())), preferred_element_type=F32)


def lay_a(recv, keys, values):
    for s in range(SEQ):
        keys[s * VT:(s + 1) * VT, :] = recv[s, 1, 0:VT, :]
        values[s * VT:(s + 1) * VT, 0:HD] = recv[s, 2, 0:VT, :]
        keys[VID + s * TT:VID + (s + 1) * TT, :] = recv[s, 1, VT:VT + TT, :]
        values[VID + s * TT:VID + (s + 1) * TT, 0:HD] = recv[s, 2, VT:VT + TT, :]
    values[:, HD:] = jnp.ones((N, HD), BF16)


def lay_c(recv, other, keys, values):
    first, tail = VT + TT, VT + TT + HALF
    for s in range(SEQ):
        at, far = s * HALF, VID // 2 + s * HALF
        keys[at:at + HALF, :] = recv[s, 1, first:tail, :]
        values[at:at + HALF, 0:HD] = recv[s, 2, first:tail, :]
        keys[far:far + HALF, :] = other[s, 0]
        values[far:far + HALF, 0:HD] = other[s, 1]
        keys[VID + s * TT:VID + (s + 1) * TT, :] = recv[s, 1, tail:ROWS, :]
        values[VID + s * TT:VID + (s + 1) * TT, 0:HD] = recv[s, 2, tail:ROWS, :]
    values[:, HD:] = jnp.ones((N, HD), BF16)


def score_chunk(query, keys, bias, scores, slot, c, top):
    rows = query.shape[0]
    s = rows_dot(query, keys[c:c + CHUNK, :])
    if c >= VID:
        s = s + bias[:, c - VID:c - VID + CHUNK]
    scores[slot, 0:rows, c:c + CHUNK] = s
    for t in range(0, CHUNK, HD):
        x = s[:, t:t + HD]
        top = x if top is None else jnp.maximum(top, x)
    return top


def keep_top(tops, slot, top):
    rows = top.shape[0]
    highest = jnp.max(top, axis=1, keepdims=True) * SCALE
    tops[slot, 0:rows, :] = jnp.broadcast_to(highest, (rows, HD))


def score_block(query, keys, bias, scores, tops, slot):
    top = None
    for c in range(0, N, CHUNK):
        top = score_chunk(query, keys, bias, scores, slot, c, top)
    keep_top(tops, slot, top)


def attend_block(rows, values, scores, tops, slot, following=None):
    highest = jnp.concatenate([tops[slot, 0:rows, :]] * (CHUNK // HD), axis=1)
    top, total = None, None
    for c in range(0, N, CHUNK):
        if following is not None:
            query, keys, bias = following
            top = score_chunk(query, keys, bias, scores, 1 - slot, c, top)
        p = jnp.exp2(scores[slot, 0:rows, c:c + CHUNK] * SCALE - highest)
        part = jnp.dot(p.astype(BF16), values[c:c + CHUNK, :], preferred_element_type=F32)
        total = part if total is None else total + part
    if following is not None:
        keep_top(tops, 1 - slot, top)
    return (total[:, 0:HD] / total[:, HD:]).astype(BF16)


def put_text(out, at, got):
    got = got.reshape(4, 4, TT, HD)
    for s in range(SEQ):
        for y in range(4):
            out[s, at + y * TT:at + (y + 1) * TT, :] = got[y, s % 4]


def text_kernel(bias_a, bias_c, recv, other, out, token, scores, tops, keys_a, values_a, keys_c, values_c):
    lay_a(recv, keys_a, values_a)
    ba, bc = bias_a[...], bias_c[...]
    score_block(recv[:, 0, VT:VT + TT, :].reshape(TXT, HD), keys_a, ba, scores, tops, 0)
    lay_c(recv, other, keys_c, values_c)
    query = recv[:, 0, VT + TT + HALF:ROWS, :].reshape(TXT, HD)
    got = attend_block(TXT, values_a, scores, tops, 0, (query, keys_c, bc))
    put_text(out, 0, got)
    put_text(out, 4 * TT, attend_block(TXT, values_c, scores, tops, 1))
    token[...] = jnp.zeros_like(token)


def video_blocks(count, rows, load, store, keys, values, bias, scores, tops):
    def step(i, slot, more):
        following = (load(i + 1), keys, bias) if more else None
        store(i, attend_block(rows, values, scores, tops, slot, following))

    score_block(load(0), keys, bias, scores, tops, 0)

    def body(j, carry):
        step(2 * j, 0, True)
        step(2 * j + 1, 1, True)
        return carry

    lax.fori_loop(0, count // 2 - 1, body, 0)
    step(count - 2, 0, True)
    step(count - 1, 1, False)


def a_kernel(bias_a, recv, _, out, token, scores, tops, keys, values):
    lay_a(recv, keys, values)

    def load(i):
        return recv[pl.ds(2 * i, 2), 0, 0:VT, :].reshape(2 * VT, HD)

    def store(i, got):
        out[pl.ds(2 * i, 2)] = got.reshape(2, VT, HD)

    video_blocks(8, 2 * VT, load, store, keys, values, bias_a[...], scores, tops)
    token[...] = jnp.zeros_like(token)


def c_kernel(bias_c, recv, other, out_a, _, out, token, scores, tops, keys, values):
    out[:, 0:VT, :] = out_a[...]
    token[...] = jnp.zeros_like(token)
    lay_c(recv, other, keys, values)

    def load(i):
        return recv[pl.ds(4 * i, 4), 0, VT + TT:VT + TT + HALF, :].reshape(4 * HALF, HD)

    def store(i, got):
        out[pl.ds(4 * i, 4), VT:, :] = got.reshape(4, HALF, HD)

    video_blocks(4, 4 * HALF, load, store, keys, values, bias_c[...], scores, tops)


def list_ranks(live, ranks):
    def body(h, count):
        alive = live[h] > 0
        ranks[h] = jnp.where(alive, count, -1)
        return count + jnp.where(alive, 1, 0)

    lax.fori_loop(0, SLOTS, body, jnp.int32(0))


def slot_text_kernel(live, core, seat, got, *rest):
    out, token, ranks = rest[-3:]
    token[...] = jnp.zeros_like(token)
    list_ranks(live, ranks)
    y, x = seat[0] // 4, seat[0] % 4
    for k in range(8):
        rank = ranks[8 * y + k]
        cols = pl.ds(pl.multiple_of((((k // 2) ^ x) * 2 + k % 2) * HD, HD), HD)
        source = jnp.where(rank < 16, jnp.clip(rank, 0, 15), 2 * jnp.clip(rank - 16, 0, 7) + core[0])
        base = jnp.where(rank < 16, 0, 4 * TT)
        for j in range(4):
            block = got[source, pl.ds(pl.multiple_of(base + (j ^ y) * TT, TT), TT), :]
            out[j * TT:(j + 1) * TT, cols] = jnp.where(rank >= 0, block, jnp.zeros_like(block))


def project_kernel(near, far, w0, w1, w2, w3, c0, c1, c2, c3, p0, p1, p2, p3, g0, g1, g2, g3, rows, cot):
    for z in range(4):
        rows[z * 128:z * 128 + 64, :] = near[z]
        rows[z * 128 + 64:(z + 1) * 128, :] = far[z]
    for w in range(8):
        for j, ref in enumerate((c0, c1, c2, c3)):
            at = (w * 4 + j) * TT
            cot[at:at + TT, :] = ref[w * TT:(w + 1) * TT, :]
    part = None
    for j, ref in enumerate((w0, w1, w2, w3)):
        term = jnp.dot(rows[:, j * 256:(j + 1) * 256], ref[...], preferred_element_type=F32)
        part = term if part is None else part + term
    part = part.reshape(8, 4, TT, 384)
    for j, ref in enumerate((p0, p1, p2, p3)):
        ref[...] = part[:, j].astype(ref.dtype)
    for j, ref in enumerate((g0, g1, g2, g3)):
        term = lax.dot_general(
            rows[:, j * 256:(j + 1) * 256], cot[...], (((0,), (0,)), ((), ())),
            preferred_element_type=F32)
        ref[...] = term.astype(ref.dtype)


def slot_video_kernel(live, core, got, other, out, slots):
    list_live(live, slots)
    mine = pl.multiple_of(core[0] * HALF, 16)
    far = pl.multiple_of((1 - core[0]) * HALF, 16)
    for r in range(16):
        out[:, head_columns(slots, r)] = got[r, 0:VT, :]
    for j in range(8):
        cols = head_columns(slots, 16 + j)
        out[pl.ds(mine, HALF), cols] = got[2 * j + core[0], VT:, :]
        out[pl.ds(far, HALF), cols] = other[j]
        out[:, head_columns(slots, LIVE + j)] = jnp.zeros((VT, HD), BF16)


def shape(*dims, dtype=BF16):
    return jax.ShapeDtypeStruct(dims, dtype)


def cost(rows):
    return pl.CostEstimate(
        flops=4 * rows * N * HD, bytes_accessed=8 << 20, transcendentals=rows * N)


def attention_call(kernel, name, rows, block, heads, out_shape, specs):
    scratch = [pltpu.VMEM((2, block, N), F32), pltpu.VMEM((2, block, HD), F32)]
    for _ in range(heads):
        scratch += [pltpu.VMEM((N, HD), BF16), pltpu.VMEM((N, 2 * HD), BF16)]
    return pl.pallas_call(
        kernel, out_shape=[out_shape, shape(8, HD, dtype=F32)], in_specs=specs,
        out_specs=[VMEM, VMEM], scratch_shapes=scratch,
        cost_estimate=cost(rows), name=name,
        compiler_params=pltpu.CompilerParams(vmem_limit_bytes=22 << 20))


def trade(x, axis, mask):
    count = 8 if axis == "dp" else SEQ
    return lax.ppermute(x, axis, [(i, i ^ mask) for i in range(count)])


def swap(x):
    return trade(x, "dp", 1)


def by_xor(x, index):
    count, rest = x.shape[0], x.shape[1:]
    bits = count.bit_length() - 1
    for b in range(bits):
        parts = x.reshape((count >> (b + 1), 2, 1 << b) + rest)
        x = jnp.where((index >> b) & 1 > 0, parts[:, ::-1], parts).reshape((count,) + rest)
    return x


def direct4(x, axis, low):
    return [x] + [trade(x, axis, j * low) for j in (1, 2, 3)]


def exchange_round(x, b):
    rest = x.shape[1:]
    parts = x.reshape((8 >> (b + 1), 2, 1 << b) + rest)
    got = trade(parts[:, 1], "dp", 1 << b)
    return jnp.stack([parts[:, 0], got], axis=1).reshape((8,) + rest)


def on_device(video_projected, text_projected, head_live, text_valid, text_weight, text_cotangent):
    video = video_projected[0].transpose(1, 0, 2)
    text = text_projected[0].transpose(1, 0, 2)
    seq = lax.axis_index("seq")
    dp = lax.axis_index("dp")
    core_bit = dp % 2
    core = core_bit.astype(jnp.int32).reshape(1)
    seat = seq.astype(jnp.int32).reshape(1)

    slots_scratch = pltpu.SMEM((SLOTS,), jnp.int32)
    give = pl.pallas_call(
        give_kernel, out_shape=shape(8, 3, HALF + TT, HD), in_specs=[SMEM, SMEM, ANY, ANY],
        out_specs=VMEM, scratch_shapes=[slots_scratch, pltpu.SemaphoreType.DMA((2,))], name="give",
        cost_estimate=pl.CostEstimate(flops=0, bytes_accessed=2 << 20, transcendentals=0),
    )(head_live, core, video, text)
    got = swap(give)
    valid_other = swap(text_valid)
    buf = pl.pallas_call(
        pack_kernel, out_shape=shape(SEQ, 3, ROWS, HD), in_specs=[SMEM, SMEM, VMEM, VMEM],
        out_specs=VMEM, scratch_shapes=[slots_scratch, pltpu.SemaphoreType.DMA((4,))], name="pack",
        cost_estimate=pl.CostEstimate(flops=0, bytes_accessed=7 << 20, transcendentals=0),
        compiler_params=pltpu.CompilerParams(vmem_limit_bytes=24 << 20),
    )(head_live, core, video, text)
    cot = by_xor(text_cotangent[0].reshape(TT, 8, 384).transpose(1, 0, 2), dp)
    cot = exchange_round(exchange_round(cot, 2), 1)
    buf, cot = lax.optimization_barrier((buf, cot))
    cot = exchange_round(cot, 0).reshape(8 * TT, 384)
    buf = pl.pallas_call(
        fill_kernel, out_shape=shape(SEQ, 3, ROWS, HD), in_specs=[SMEM, VMEM, ANY],
        out_specs=ANY, scratch_shapes=[pltpu.SemaphoreType.DMA], name="fill",
        input_output_aliases={2: 0},
    )(core, got, buf)
    buf, valid_other, cot = lax.optimization_barrier((buf, valid_other, cot))
    recv = lax.all_to_all(buf, "seq", split_axis=0, concat_axis=0, tiled=True)
    other = swap(recv[:, 1:3, VT + TT:VT + TT + HALF, :])

    bias_a = jnp.where(text_valid > 0, 0.0, -1e30).astype(F32)
    bias_far = jnp.where(valid_other > 0, 0.0, -1e30).astype(F32)
    bias_c = jnp.where(seq % 2 == core_bit, bias_a, bias_far)

    text_out, token = attention_call(
        text_kernel, "text_attention", 2 * TXT, TXT, 2, shape(SEQ, 8 * TT, HD), [VMEM] * 4,
    )(bias_a, bias_c, recv, other)
    text_out, weight, cot = lax.optimization_barrier((text_out, text_weight, cot))
    weight_x = direct4(weight, "seq", 1)
    cot_y = direct4(cot, "seq", 4)
    text_got = lax.all_to_all(text_out, "seq", split_axis=0, concat_axis=0, tiled=True)

    out_a, token = attention_call(
        a_kernel, "video_attention_a", VID, 2 * VT, 1, shape(SEQ, VT, HD), [VMEM] * 3,
    )(bias_a, recv, token)
    text_rows, token = pl.pallas_call(
        slot_text_kernel, out_shape=[shape(4 * TT, 8 * HD), shape(8, HD, dtype=F32)],
        in_specs=[SMEM, SMEM, SMEM, VMEM, VMEM] + [ANY] * 6, out_specs=[VMEM, VMEM],
        scratch_shapes=[slots_scratch],
        name="slot_text",
    )(head_live, core, seat, text_got, token, *weight_x[1:], *cot_y[1:])
    out_c, _ = attention_call(
        c_kernel, "video_attention_c", VID // 2, 4 * HALF, 1, shape(SEQ, VT + HALF, HD),
        [VMEM] * 5,
    )(bias_c, recv, other, out_a, token)
    rows_near = jnp.stack(direct4(text_rows, "dp", 2))
    out_c, rows_near = lax.optimization_barrier((out_c, rows_near))
    back = lax.all_to_all(out_c, "seq", split_axis=0, concat_axis=0, tiled=True)
    rows_far = swap(rows_near)
    sums = pl.pallas_call(
        project_kernel,
        out_shape=[shape(8, TT, 384, dtype=F32)] + [shape(8, TT, 384)] * 3
        + [shape(256, 384, dtype=F32)] + [shape(256, 384)] * 3,
        in_specs=[VMEM] * 10, out_specs=[VMEM] * 8, name="project",
        scratch_shapes=[pltpu.VMEM((512, 8 * HD), BF16), pltpu.VMEM((512, 384), BF16)],
        compiler_params=pltpu.CompilerParams(vmem_limit_bytes=20 << 20),
    )(rows_near, rows_far, *weight_x, *cot_y)
    projected = sums[0]
    for j in (1, 2, 3):
        projected = projected + trade(sums[j], "seq", 4 * j).astype(F32)
    gradient = sums[4]
    for j in (1, 2, 3):
        gradient = gradient + trade(sums[4 + j], "seq", j).astype(F32)
    projected, back = lax.optimization_barrier((projected.astype(BF16), back))
    halves = swap(lax.dynamic_index_in_dim(
        back.reshape(8, 2, VT + HALF, HD)[:, :, VT:], 1 - core_bit, 1, keepdims=False))
    video_attended = pl.pallas_call(
        slot_video_kernel, out_shape=shape(VT, SLOTS * HD), in_specs=[SMEM, SMEM] + [VMEM] * 2,
        out_specs=VMEM, scratch_shapes=[slots_scratch], name="slot_video",
    )(head_live, core, back, halves)

    projected = exchange_round(projected, 2)
    projected = by_xor(exchange_round(exchange_round(projected, 1), 0), dp)
    text_output = projected.transpose(1, 0, 2).reshape(TT, 8 * 384)
    return (video_attended[None], text_output[None], gradient)


def solution(mesh):
    in_specs = (
        P("dp", "seq", None, None),
        P("dp", "seq", None, None),
        P(),
        P("dp", None),
        P("seq", "dp"),
        P("dp", "seq", None),
    )
    out_specs = (P("dp", "seq", None), P("dp", "seq", None), P("seq", "dp"))
    return jax.shard_map(
        on_device, mesh=mesh, in_specs=in_specs, out_specs=out_specs, check_vma=False
    )
```
